32 devices in a mesh: prow: 2 (over core), pcol: 16 (over z, y, x).
Axes of the slice: x: 2, y: 2, z: 4, core: 2. Of those that a mesh axis runs over, the one named last changes fastest.
Arguments:
- slab: float32 [1024, 98304], P('pcol', 'prow'), may hold values from -6 to 6
- vectors: float32 [98304, 512], P(('prow', 'pcol')), may hold values from -0.01953125 to 0.01953125
- tfactors: float32 [4, 128, 128], replicated, as said below
Outputs:
- transformed: float32 [1024, 98304], P('pcol', 'prow')
The draws below stay inside these ranges and needn't reach their ends.
Inputs may be any that keep to these rules, and one draw needn't show every extreme that they name: Each tfactors[k] is upper triangular with diagonal entries between 1 and 2.
All inputs are finite; a program needn't handle non-finite values.
Results may differ from the reference program's by a relative error of at most 0.0001.
Values sent between devices are 32-bit elements; how exact they have to be, the bound alone decides.
A program may use at most 192 MiB of HBM per device.

```python
import jax
import jax.numpy as jnp
from jax import lax

N = 98304
NB = 128
NBLK = 4
M = 1024


def draw_tfactors(key, part):
    key_diag, key_off = jax.random.split(key)
    diag_vals = jax.random.uniform(key_diag, (NBLK, NB), jnp.float32, 1.0, 2.0)
    off_vals = jax.random.normal(key_off, (NBLK, NB, NB), jnp.float32) * (0.5 * NB ** (-0.5))
    upper = jnp.triu(off_vals, 1)
    return upper + diag_vals[:, :, None] * jnp.eye(NB, dtype=jnp.float32)[None, :, :]


def steps_of(own_key, dims, shards, least, top_value):
    loudness = 1.0
    for position, shards_of in shards:
        draws = jax.random.uniform(jax.random.fold_in(jax.random.fold_in(own_key, 6), position), (shards_of,), jnp.float32, least / len(shards), top_value / len(shards))
        loudness = loudness * jnp.repeat(jnp.exp(draws), dims[position] // shards_of).reshape((-1,) + (1,) * (len(dims) - 1 - position))
    return loudness


def bell_draw(key, shape, spread, bound, cuts=(), held_as=jnp.bfloat16):
    result = jax.random.normal(key, shape, jnp.float32) * spread
    if len(cuts) > 0:
        result = steps_of(key, shape, cuts, -0.22, 0.18) * result
    return jnp.clip(result, min=-bound, max=bound).astype(held_as)


def setup_inputs(seed: int = 0) -> dict:
    splits = jax.random.split(jax.random.key(seed), 4)
    return {
        "slab": bell_draw(splits[0], (M, N), 1.0, 6.0, ((0, 16), (1, 2)), jnp.float32),
        "vectors": bell_draw(splits[1], (N, NB * NBLK), N ** -0.5, 0.01953125, ((0, 32),), jnp.float32),
        "tfactors": draw_tfactors(jax.random.fold_in(splits[3], 71), 0),
    }


def reference(slab, vectors, tfactors):
    transformed = slab
    for k in reversed(range(NBLK)):
        block = vectors[:, k * NB:(k + 1) * NB]
        part = jnp.dot(transformed, block, precision=lax.Precision.HIGHEST, preferred_element_type=jnp.float32)
        scaled = jnp.dot(part, tfactors[k].T, precision=lax.Precision.HIGHEST, preferred_element_type=jnp.float32)
        transformed = transformed - jnp.dot(scaled, block.T, precision=lax.Precision.HIGHEST, preferred_element_type=jnp.float32)
    return transformed
```

```python
import functools

import jax
import jax.numpy as jnp
from jax import lax
from jax.experimental import pallas as pl
from jax.experimental.pallas import tpu as pltpu
from jax.sharding import PartitionSpec as P

MESH = pl.DeviceIdType.MESH
GROUP = 4
CHUNKS = 4


def matmul(left, right, precision=lax.Precision.HIGHEST):
    return jnp.dot(left, right, precision=precision, preferred_element_type=jnp.float32)


def greet_all(count):
    row, me = lax.axis_index("prow"), lax.axis_index("pcol")
    barrier = pltpu.get_barrier_semaphore()
    for step in range(1, count):
        pl.semaphore_signal(barrier, inc=1, device_id=(row, lax.rem(me + step, count)), device_id_type=MESH)
    pl.semaphore_wait(barrier, count - 1)


def place_of(line, plane, piece):
    reach = line - 2
    return jnp.clip(plane, piece - reach, piece + reach)


def spread_kernel(line, slab_ref, vec_ref, xr, vall, xsend, xrecv, vright, vleft, vrecv, own_sem):
    count = line * GROUP
    row, me = lax.axis_index("prow"), lax.axis_index("pcol")
    z, q = me // GROUP, lax.rem(me, GROUP)
    depth = vec_ref.shape[0]
    part = depth // CHUNKS
    greet_all(count)

    def vcopy(source, chunk, to, src, sems):
        rows = pl.ds(chunk * part, part)
        return pltpu.make_async_remote_copy(
            src_ref=src.at[rows, :],
            dst_ref=vall.at[source, rows, :],
            send_sem=sems.at[source, chunk],
            recv_sem=vrecv.at[source, chunk],
            device_id=(row, to * GROUP + q),
            device_id_type=MESH,
        )

    for chunk in range(CHUNKS):
        @pl.when(z < line - 1)
        def _():
            vcopy(z, chunk, z + 1, vec_ref, vright).start()

        @pl.when(z > 0)
        def _():
            vcopy(z, chunk, z - 1, vec_ref, vleft).start()

    own = pltpu.make_async_copy(vec_ref, vall.at[z], own_sem)
    own.start()

    def xcopy(piece, step):
        other = lax.rem(q + step, GROUP)
        place = place_of(line, z, piece)
        slot = jnp.where(place == z, piece, line)
        columns = pl.ds(pl.multiple_of((piece * GROUP + other) * depth, 128), depth)
        return place, other, slot, columns

    def xremote(piece, step):
        place, other, slot, columns = xcopy(piece, step)
        return pltpu.make_async_remote_copy(
            src_ref=slab_ref.at[:, columns],
            dst_ref=xr.at[slot, q],
            send_sem=xsend.at[piece, step],
            recv_sem=xrecv.at[slot, q],
            device_id=(row, place * GROUP + other),
            device_id_type=MESH,
        )

    def xlocal(piece):
        _, _, _, columns = xcopy(piece, 0)
        return pltpu.make_async_copy(slab_ref.at[:, columns], xr.at[piece, q], xrecv.at[piece, q])

    def far(piece):
        return place_of(line, z, piece) != z

    for step in (1, 2, 3, 0):
        for piece in range(line):
            if step:
                xremote(piece, step).start()
            else:
                @pl.when(far(piece))
                def _():
                    xremote(piece, 0).start()

                @pl.when(jnp.logical_not(far(piece)))
                def _():
                    xlocal(piece).start()

    for distance in range(1, line - 1):
        for chunk in range(CHUNKS):
            @pl.when(z - distance >= 0)
            def _():
                source = z - distance
                vcopy(source, chunk, z, vall.at[source], vright).wait_recv()
                if distance + 1 <= line - 2:
                    @pl.when(z < line - 1)
                    def _():
                        vcopy(source, chunk, z + 1, vall.at[source], vright).start()

            @pl.when(z + distance <= line - 1)
            def _():
                source = z + distance
                vcopy(source, chunk, z, vall.at[source], vleft).wait_recv()
                if distance + 1 <= line - 2:
                    @pl.when(z > 0)
                    def _():
                        vcopy(source, chunk, z - 1, vall.at[source], vleft).start()

    own.wait()

    def xarrived(slot, other):
        pltpu.make_async_remote_copy(
            src_ref=xr.at[slot, other],
            dst_ref=xr.at[slot, other],
            send_sem=xsend.at[0, 0],
            recv_sem=xrecv.at[slot, other],
            device_id=(row, me),
            device_id_type=MESH,
        ).wait_recv()

    for piece in range(line):
        @pl.when(jnp.logical_not(far(piece)))
        def _():
            xlocal(piece).wait()
            for step in range(1, GROUP):
                xarrived(piece, lax.rem(q + step, GROUP))

    @pl.when(jnp.logical_or(z == 1, z == line - 2))
    def _():
        for other in range(GROUP):
            xarrived(line, other)

    for piece in range(line):
        for step in range(1, GROUP):
            xremote(piece, step).wait_send()

        @pl.when(far(piece))
        def _():
            xremote(piece, 0).wait_send()

    for distance in range(0, line - 2):
        for chunk in range(CHUNKS):
            @pl.when(jnp.logical_and(z - distance >= 0, z < line - 1))
            def _():
                vcopy(z - distance, chunk, z + 1, vec_ref, vright).wait_send()

            @pl.when(jnp.logical_and(z + distance <= line - 1, z > 0))
            def _():
                vcopy(z + distance, chunk, z - 1, vec_ref, vleft).wait_send()


def spread(line, slab, vectors):
    rows = slab.shape[0]
    depth, width = vectors.shape
    return pl.pallas_call(
        functools.partial(spread_kernel, line),
        out_shape=(
            jax.ShapeDtypeStruct((line + 1, GROUP, rows, depth), jnp.float32),
            jax.ShapeDtypeStruct((line, depth, width), jnp.float32),
        ),
        in_specs=[pl.BlockSpec(memory_space=pl.ANY)] * 2,
        out_specs=(pl.BlockSpec(memory_space=pl.ANY),) * 2,
        scratch_shapes=[
            pltpu.SemaphoreType.DMA((line, GROUP)),
            pltpu.SemaphoreType.DMA((line + 1, GROUP)),
            pltpu.SemaphoreType.DMA((line, CHUNKS)),
            pltpu.SemaphoreType.DMA((line, CHUNKS)),
            pltpu.SemaphoreType.DMA((line, CHUNKS)),
            pltpu.SemaphoreType.DMA,
        ],
        compiler_params=pltpu.CompilerParams(collective_id=0, has_side_effects=True),
        name="spread",
    )(slab, vectors)


def give_back_kernel(line, c_ref, out_ref, send, recv):
    count = line * GROUP
    row, me = lax.axis_index("prow"), lax.axis_index("pcol")
    z, q = me // GROUP, lax.rem(me, GROUP)
    depth = c_ref.shape[3]
    greet_all(count)

    def columns(piece, other):
        return pl.ds(pl.multiple_of((piece * GROUP + other) * depth, 128), depth)

    def remote(slot, piece, plane, other):
        return pltpu.make_async_remote_copy(
            src_ref=c_ref.at[slot, other],
            dst_ref=out_ref.at[:, columns(piece, q)],
            send_sem=send.at[slot, other],
            recv_sem=recv.at[piece, q],
            device_id=(row, plane * GROUP + other),
            device_id_type=MESH,
        )

    def local(piece):
        return pltpu.make_async_copy(c_ref.at[piece, q], out_ref.at[:, columns(piece, q)], recv.at[piece, q])

    def near(piece):
        return place_of(line, z, piece) == z

    helps = jnp.logical_or(z == 1, z == line - 2)
    far_plane = jnp.where(z == 1, 0, line - 1)
    far_piece = jnp.where(z == 1, line - 1, 0)

    @pl.when(helps)
    def _():
        for other in range(GROUP):
            remote(line, far_piece, far_plane, other).start()

    for step in (1, 2, 3, 0):
        for piece in range(line):
            @pl.when(near(piece))
            def _():
                if step:
                    remote(piece, piece, z, lax.rem(q + step, GROUP)).start()
                else:
                    local(piece).start()

    def arrived(piece, other):
        pltpu.make_async_remote_copy(
            src_ref=c_ref.at[0, 0],
            dst_ref=out_ref.at[:, columns(piece, other)],
            send_sem=send.at[0, 0],
            recv_sem=recv.at[piece, other],
            device_id=(row, me),
            device_id_type=MESH,
        ).wait_recv()

    for piece in range(line):
        for step in range(1, GROUP):
            arrived(piece, lax.rem(q + step, GROUP))

        @pl.when(near(piece))
        def _():
            local(piece).wait()

        @pl.when(jnp.logical_not(near(piece)))
        def _():
            arrived(piece, q)

    for piece in range(line):
        @pl.when(near(piece))
        def _():
            for step in range(1, GROUP):
                remote(piece, piece, z, lax.rem(q + step, GROUP)).wait_send()

    @pl.when(helps)
    def _():
        for other in range(GROUP):
            remote(line, far_piece, far_plane, other).wait_send()


def give_back(line, correction):
    _, _, rows, depth = correction.shape
    return pl.pallas_call(
        functools.partial(give_back_kernel, line),
        out_shape=jax.ShapeDtypeStruct((rows, line * GROUP * depth), jnp.float32),
        in_specs=[pl.BlockSpec(memory_space=pl.ANY)],
        out_specs=pl.BlockSpec(memory_space=pl.ANY),
        scratch_shapes=[
            pltpu.SemaphoreType.DMA((line + 1, GROUP)),
            pltpu.SemaphoreType.DMA((line, GROUP)),
        ],
        compiler_params=pltpu.CompilerParams(collective_id=1, has_side_effects=True),
        name="give_back",
    )(correction)


def per_device(line, slab, vectors, tfactors):
    count, width = tfactors.shape[0], tfactors.shape[1]
    rows = slab.shape[0]
    depth, total = vectors.shape
    z = lax.axis_index("pcol") // GROUP
    high = lax.Precision.HIGH

    gram = lax.psum(matmul(vectors.T, vectors, high), ("prow", "pcol"))
    xr, vall = spread(line, slab, vectors)
    xr = xr.reshape(line + 1, GROUP * rows, depth)

    own = jnp.zeros((GROUP * rows, total), jnp.float32)
    for piece in range(line):
        near = place_of(line, z, piece) == z
        own = own + jnp.where(near, matmul(xr[piece], vall[piece], high), 0.0)
    helps = jnp.logical_or(z == 1, z == line - 2)
    far_plane = jnp.where(z == 1, 0, line - 1)
    far_piece = jnp.where(z == 1, line - 1, 0)
    far_vectors = lax.dynamic_index_in_dim(vall, far_piece, 0, keepdims=False)
    extra = jnp.where(helps, matmul(xr[line], far_vectors, high), 0.0)

    products = jnp.zeros((line, GROUP * rows, total), jnp.float32)
    products = lax.dynamic_update_index_in_dim(products, own, z, 0)
    before = lax.dynamic_index_in_dim(products, far_plane, 0, keepdims=False)
    products = lax.dynamic_update_index_in_dim(products, jnp.where(helps, extra, before), far_plane, 0)
    products = lax.psum(products, ("prow", "pcol"))

    def weights(part):
        done = {}
        for k in reversed(range(count)):
            now = part[:, k * width : (k + 1) * width]
            for j in done:
                now = now - matmul(done[j], gram[j * width : (j + 1) * width, k * width : (k + 1) * width])
            done[k] = matmul(now, tfactors[k].T)
        return jnp.concatenate([done[k] for k in range(count)], axis=1)

    both = jnp.concatenate([
        lax.dynamic_index_in_dim(products, z, 0, keepdims=False),
        lax.dynamic_index_in_dim(products, far_plane, 0, keepdims=False),
    ])
    both = weights(both)
    w_own, w_far = both[: GROUP * rows], both[GROUP * rows :]
    parts = [matmul(w_own, vall[piece].T, high) for piece in range(line)]
    parts.append(matmul(w_far, far_vectors.T, high))
    correction = jnp.stack(parts).reshape(line + 1, GROUP, rows, depth)
    return slab - give_back(line, correction)


def solution(mesh):
    line = mesh.shape["pcol"] // GROUP
    in_specs = (P("pcol", "prow"), P(("prow", "pcol"), None), P())
    out_specs = P("pcol", "prow")
    return jax.shard_map(
        functools.partial(per_device, line), mesh=mesh, in_specs=in_specs, out_specs=out_specs, check_vma=False
    )
```

```python
import functools

import jax
import jax.numpy as jnp
from jax import lax
from jax.experimental import pallas as pl
from jax.experimental.pallas import tpu as pltpu
from jax.sharding import PartitionSpec as P

MESH = pl.DeviceIdType.MESH
GROUP = 4
CHUNKS = 4


def matmul(left, right, precision=lax.Precision.HIGHEST):
    return jnp.dot(left, right, precision=precision, preferred_element_type=jnp.float32)


def greet_all(count):
    row, me = lax.axis_index("prow"), lax.axis_index("pcol")
    barrier = pltpu.get_barrier_semaphore()
    for step in range(1, count):
        pl.semaphore_signal(barrier, inc=1, device_id=(row, lax.rem(me + step, count)), device_id_type=MESH)
    pl.semaphore_wait(barrier, count - 1)


def place_of(line, plane, piece):
    reach = line - 2
    return jnp.clip(plane, piece - reach, piece + reach)


def spread_kernel(line, slab_ref, vec_ref, xr, vall, xsend, xrecv, vright, vleft, vrecv, own_sem):
    count = line * GROUP
    row, me = lax.axis_index("prow"), lax.axis_index("pcol")
    z, q = me // GROUP, lax.rem(me, GROUP)
    depth = vec_ref.shape[0]
    part = depth // CHUNKS
    greet_all(count)

    def vcopy(source, chunk, to, src, sems):
        rows = pl.ds(chunk * part, part)
        return pltpu.make_async_remote_copy(
            src_ref=src.at[rows, :],
            dst_ref=vall.at[source, rows, :],
            send_sem=sems.at[source, chunk],
            recv_sem=vrecv.at[source, chunk],
            device_id=(row, to * GROUP + q),
            device_id_type=MESH,
        )

    for chunk in range(CHUNKS):
        @pl.when(z < line - 1)
        def _():
            vcopy(z, chunk, z + 1, vec_ref, vright).start()

        @pl.when(z > 0)
        def _():
            vcopy(z, chunk, z - 1, vec_ref, vleft).start()

    own = pltpu.make_async_copy(vec_ref, vall.at[z], own_sem)
    own.start()

    def xcopy(piece, step):
        other = lax.rem(q + step, GROUP)
        place = place_of(line, z, piece)
        slot = jnp.where(place == z, piece, line)
        columns = pl.ds(pl.multiple_of((piece * GROUP + other) * depth, 128), depth)
        return place, other, slot, columns

    def xremote(piece, step):
        place, other, slot, columns = xcopy(piece, step)
        return pltpu.make_async_remote_copy(
            src_ref=slab_ref.at[:, columns],
            dst_ref=xr.at[slot, q],
            send_sem=xsend.at[piece, step],
            recv_sem=xrecv.at[slot, q],
            device_id=(row, place * GROUP + other),
            device_id_type=MESH,
        )

    def xlocal(piece):
        _, _, _, columns = xcopy(piece, 0)
        return pltpu.make_async_copy(slab_ref.at[:, columns], xr.at[piece, q], xrecv.at[piece, q])

    def far(piece):
        return place_of(line, z, piece) != z

    for step in (1, 2, 3, 0):
        for piece in range(line):
            if step:
                xremote(piece, step).start()
            else:
                @pl.when(far(piece))
                def _():
                    xremote(piece, 0).start()

                @pl.when(jnp.logical_not(far(piece)))
                def _():
                    xlocal(piece).start()

    for distance in range(1, line - 1):
        for chunk in range(CHUNKS):
            @pl.when(z - distance >= 0)
            def _():
                source = z - distance
                vcopy(source, chunk, z, vall.at[source], vright).wait_recv()
                if distance + 1 <= line - 2:
                    @pl.when(z < line - 1)
                    def _():
                        vcopy(source, chunk, z + 1, vall.at[source], vright).start()

            @pl.when(z + distance <= line - 1)
            def _():
                source = z + distance
                vcopy(source, chunk, z, vall.at[source], vleft).wait_recv()
                if distance + 1 <= line - 2:
                    @pl.when(z > 0)
                    def _():
                        vcopy(source, chunk, z - 1, vall.at[source], vleft).start()

    own.wait()

    def xarrived(slot, other):
        pltpu.make_async_remote_copy(
            src_ref=xr.at[slot, other],
            dst_ref=xr.at[slot, other],
            send_sem=xsend.at[0, 0],
            recv_sem=xrecv.at[slot, other],
            device_id=(row, me),
            device_id_type=MESH,
        ).wait_recv()

    for piece in range(line):
        @pl.when(jnp.logical_not(far(piece)))
        def _():
            xlocal(piece).wait()
            for step in range(1, GROUP):
                xarrived(piece, lax.rem(q + step, GROUP))

    @pl.when(jnp.logical_or(z == 1, z == line - 2))
    def _():
        for other in range(GROUP):
            xarrived(line, other)

    for piece in range(line):
        for step in range(1, GROUP):
            xremote(piece, step).wait_send()

        @pl.when(far(piece))
        def _():
            xremote(piece, 0).wait_send()

    for distance in range(0, line - 2):
        for chunk in range(CHUNKS):
            @pl.when(jnp.logical_and(z - distance >= 0, z < line - 1))
            def _():
                vcopy(z - distance, chunk, z + 1, vec_ref, vright).wait_send()

            @pl.when(jnp.logical_and(z + distance <= line - 1, z > 0))
            def _():
                vcopy(z + distance, chunk, z - 1, vec_ref, vleft).wait_send()


def spread(line, slab, vectors):
    rows = slab.shape[0]
    depth, width = vectors.shape
    return pl.pallas_call(
        functools.partial(spread_kernel, line),
        out_shape=(
            jax.ShapeDtypeStruct((line + 1, GROUP, rows, depth), jnp.float32),
            jax.ShapeDtypeStruct((line, depth, width), jnp.float32),
        ),
        in_specs=[pl.BlockSpec(memory_space=pl.ANY)] * 2,
        out_specs=(pl.BlockSpec(memory_space=pl.ANY),) * 2,
        scratch_shapes=[
            pltpu.SemaphoreType.DMA((line, GROUP)),
            pltpu.SemaphoreType.DMA((line + 1, GROUP)),
            pltpu.SemaphoreType.DMA((line, CHUNKS)),
            pltpu.SemaphoreType.DMA((line, CHUNKS)),
            pltpu.SemaphoreType.DMA((line, CHUNKS)),
            pltpu.SemaphoreType.DMA,
        ],
        compiler_params=pltpu.CompilerParams(collective_id=0, has_side_effects=True),
        name="spread",
    )(slab, vectors)


def split(value):
    coarse = value.astype(jnp.bfloat16)
    return coarse, (value - coarse.astype(jnp.float32)).astype(jnp.bfloat16)


def across(left, right):
    return lax.dot_general(left, right, (((1,), (1,)), ((), ())), preferred_element_type=jnp.float32)


def finish_kernel(
    line, lanes, x_ref, v_ref, y_ref, gram_ref, t_ref, out_ref,
    xbuf, vbuf, inbox, total, wbox, wsplit,
    xload, vload, ysend, yrecv, wsend, wrecv, send, recv,
):
    row, me = lax.axis_index("prow"), lax.axis_index("pcol")
    z, q = me // GROUP, lax.rem(me, GROUP)
    members = lanes * GROUP
    mine = row * GROUP + q
    blocks, width = t_ref.shape[0], t_ref.shape[1]
    rows, depth = xbuf.shape[2], xbuf.shape[3]
    share = GROUP * rows // members

    helps = jnp.logical_or(z == 1, z == line - 2)
    ends = jnp.logical_or(z == 0, z == line - 1)
    low = z <= 1
    far_plane = jnp.where(low, 0, line - 1)
    far_piece = jnp.where(low, line - 1, 0)
    help_plane = jnp.where(low, 1, line - 2)
    partner = jnp.where(ends, help_plane, far_plane)

    def device(plane, member):
        return (member // GROUP, plane * GROUP + lax.rem(member, GROUP))

    def others():
        return [lax.rem(mine + step, members) for step in range(1, members)]

    for slot in range(line + 1):
        pltpu.make_async_copy(x_ref.at[slot], xbuf.at[slot], xload.at[slot]).start()
    for piece in range(line):
        pltpu.make_async_copy(v_ref.at[piece], vbuf.at[piece], vload.at[piece]).start()

    barrier = pltpu.get_barrier_semaphore()
    for other in others():
        pl.semaphore_signal(barrier, inc=1, device_id=device(z, other), device_id_type=MESH)

    @pl.when(jnp.logical_or(helps, ends))
    def _():
        for other in range(members):
            pl.semaphore_signal(barrier, inc=1, device_id=device(partner, other), device_id_type=MESH)

    pl.semaphore_wait(barrier, members - 1 + jnp.where(jnp.logical_or(helps, ends), members, 0))

    def strip(member):
        return pl.ds(pl.multiple_of(member * share, share), share)

    def ycopy(kind, plane, member):
        return pltpu.make_async_remote_copy(
            src_ref=y_ref.at[kind, strip(member), :],
            dst_ref=inbox.at[kind * members + mine],
            send_sem=ysend.at[kind * members + member],
            recv_sem=yrecv.at[kind * members + mine],
            device_id=device(plane, member),
            device_id_type=MESH,
        )

    def yarrived(index):
        pltpu.make_async_remote_copy(
            src_ref=inbox.at[index],
            dst_ref=inbox.at[index],
            send_sem=ysend.at[0],
            recv_sem=yrecv.at[index],
            device_id=(row, me),
            device_id_type=MESH,
        ).wait_recv()

    @pl.when(helps)
    def _():
        for other in range(members):
            ycopy(1, far_plane, other).start()

    for other in others():
        ycopy(0, z, other).start()

    total[...] = y_ref[0, strip(mine), :]
    for other in others():
        yarrived(other)
        total[...] += inbox[other]

    @pl.when(ends)
    def _():
        for other in range(members):
            yarrived(members + other)
            total[...] += inbox[members + other]

    done = {}
    for k in reversed(range(blocks)):
        now = total[:, k * width : (k + 1) * width]
        for j in done:
            now = now - matmul(done[j], gram_ref[j * width : (j + 1) * width, k * width : (k + 1) * width])
        done[k] = lax.dot_general(
            now, t_ref[k], (((1,), (1,)), ((), ())),
            precision=lax.Precision.HIGHEST, preferred_element_type=jnp.float32,
        )
    for k in range(blocks):
        wbox[0, strip(mine), k * width : (k + 1) * width] = done[k]

    def wcopy(kind, plane, member):
        return pltpu.make_async_remote_copy(
            src_ref=wbox.at[0, strip(mine), :],
            dst_ref=wbox.at[kind, strip(mine), :],
            send_sem=wsend.at[kind * members + member],
            recv_sem=wrecv.at[kind * members + mine],
            device_id=device(plane, member),
            device_id_type=MESH,
        )

    def warrived(kind, member):
        pltpu.make_async_remote_copy(
            src_ref=wbox.at[kind, strip(member), :],
            dst_ref=wbox.at[kind, strip(member), :],
            send_sem=wsend.at[0],
            recv_sem=wrecv.at[kind * members + member],
            device_id=(row, me),
            device_id_type=MESH,
        ).wait_recv()

    @pl.when(ends)
    def _():
        for other in range(members):
            wcopy(1, help_plane, other).start()

    for other in others():
        wcopy(0, z, other).start()

    def xarrive(slot):
        pltpu.make_async_copy(x_ref.at[slot], xbuf.at[slot], xload.at[slot]).wait()

    for slot in range(line + 1):
        xarrive(slot)
    for piece in range(line):
        pltpu.make_async_copy(v_ref.at[piece], vbuf.at[piece], vload.at[piece]).wait()

    tile = 512 if depth % 512 == 0 else depth

    def update(slot, piece, kind):
        def body(index, carry):
            span = pl.ds(pl.multiple_of(index * tile, tile), tile)
            coarse, fine = split(vbuf[piece, span, :])
            first, second = wsplit[2 * kind], wsplit[2 * kind + 1]
            change = across(first, coarse) + (across(second, coarse) + across(first, fine))
            for group in range(GROUP):
                xbuf[slot, group, :, span] = (
                    xbuf[slot, group, :, span] - change[group * rows : (group + 1) * rows]
                )
            return carry

        lax.fori_loop(0, depth // tile, body, 0)

    def columns(piece, other):
        return pl.ds(pl.multiple_of((piece * GROUP + other) * depth, 128), depth)

    def remote(slot, piece, plane, other):
        return pltpu.make_async_remote_copy(
            src_ref=xbuf.at[slot, other],
            dst_ref=out_ref.at[:, columns(piece, q)],
            send_sem=send.at[slot, other],
            recv_sem=recv.at[piece, q],
            device_id=(row, plane * GROUP + other),
            device_id_type=MESH,
        )

    def local(piece):
        return pltpu.make_async_copy(xbuf.at[piece, q], out_ref.at[:, columns(piece, q)], recv.at[piece, q])

    def near(piece):
        return place_of(line, z, piece) == z

    for other in others():
        warrived(0, other)
    wsplit[0], wsplit[1] = split(wbox[0])

    for piece in range(line):
        @pl.when(near(piece))
        def _():
            update(piece, piece, 0)
            for step in (1, 2, 3):
                remote(piece, piece, z, lax.rem(q + step, GROUP)).start()
            local(piece).start()

        if piece == 0:
            @pl.when(helps)
            def _():
                for other in range(members):
                    warrived(1, other)
                wsplit[2], wsplit[3] = split(wbox[1])
                update(line, far_piece, 1)
                for other in range(GROUP):
                    remote(line, far_piece, far_plane, other).start()

    def arrived(piece, other):
        pltpu.make_async_remote_copy(
            src_ref=xbuf.at[0, 0],
            dst_ref=out_ref.at[:, columns(piece, other)],
            send_sem=send.at[0, 0],
            recv_sem=recv.at[piece, other],
            device_id=(row, me),
            device_id_type=MESH,
        ).wait_recv()

    for piece in range(line):
        for step in range(1, GROUP):
            arrived(piece, lax.rem(q + step, GROUP))

        @pl.when(near(piece))
        def _():
            local(piece).wait()
            for step in range(1, GROUP):
                remote(piece, piece, z, lax.rem(q + step, GROUP)).wait_send()

        @pl.when(jnp.logical_not(near(piece)))
        def _():
            arrived(piece, q)

    for other in others():
        ycopy(0, z, other).wait_send()
        wcopy(0, z, other).wait_send()

    @pl.when(ends)
    def _():
        for other in range(members):
            wcopy(1, help_plane, other).wait_send()

    @pl.when(helps)
    def _():
        for other in range(members):
            ycopy(1, far_plane, other).wait_send()
        for other in range(GROUP):
            remote(line, far_piece, far_plane, other).wait_send()


def finish(line, lanes, x, v, y, gram, tfactors):
    _, _, rows, depth = x.shape
    total = v.shape[2]
    members = lanes * GROUP
    share = GROUP * rows // members
    dma = pltpu.SemaphoreType.DMA
    return pl.pallas_call(
        functools.partial(finish_kernel, line, lanes),
        out_shape=jax.ShapeDtypeStruct((rows, line * GROUP * depth), jnp.float32),
        in_specs=[pl.BlockSpec(memory_space=pl.ANY)] * 2 + [pl.BlockSpec(memory_space=pltpu.VMEM)] * 3,
        out_specs=pl.BlockSpec(memory_space=pl.ANY),
        scratch_shapes=[
            pltpu.VMEM(x.shape, jnp.float32),
            pltpu.VMEM(v.shape, jnp.float32),
            pltpu.VMEM((2 * members, share, total), jnp.float32),
            pltpu.VMEM((share, total), jnp.float32),
            pltpu.VMEM((2, GROUP * rows, total), jnp.float32),
            pltpu.VMEM((4, GROUP * rows, total), jnp.bfloat16),
            dma((line + 1,)),
            dma((line,)),
            dma((2 * members,)),
            dma((2 * members,)),
            dma((2 * members,)),
            dma((2 * members,)),
            dma((line + 1, GROUP)),
            dma((line, GROUP)),
        ],
        compiler_params=pltpu.CompilerParams(
            collective_id=1, has_side_effects=True, vmem_limit_bytes=60 * 1024 * 1024
        ),
        name="finish",
    )(x, v, y, gram, tfactors)


def per_device(line, lanes, slab, vectors, tfactors):
    rows = slab.shape[0]
    depth, total = vectors.shape
    z = lax.axis_index("pcol") // GROUP
    high = lax.Precision.HIGH

    gram = lax.psum(matmul(vectors.T, vectors, high), ("prow", "pcol"))
    blocks, vall = spread(line, slab, vectors)
    xr = blocks.reshape(line + 1, GROUP * rows, depth)

    own = jnp.zeros((GROUP * rows, total), jnp.float32)
    for piece in range(line):
        near = place_of(line, z, piece) == z
        own = own + jnp.where(near, matmul(xr[piece], vall[piece], high), 0.0)
    far_piece = jnp.where(z <= 1, line - 1, 0)
    far_vectors = lax.dynamic_index_in_dim(vall, far_piece, 0, keepdims=False)
    extra = matmul(xr[line], far_vectors, high)
    return finish(line, lanes, blocks, vall, jnp.stack([own, extra]), gram, tfactors)


def solution(mesh):
    line = mesh.shape["pcol"] // GROUP
    lanes = mesh.shape["prow"]
    in_specs = (P("pcol", "prow"), P(("prow", "pcol"), None), P())
    out_specs = P("pcol", "prow")
    return jax.shard_map(
        functools.partial(per_device, line, lanes),
        mesh=mesh, in_specs=in_specs, out_specs=out_specs, check_vma=False,
    )
```

```python
import functools

import jax
import jax.numpy as jnp
from jax import lax
from jax.experimental import pallas as pl
from jax.experimental.pallas import tpu as pltpu
from jax.sharding import PartitionSpec as P

MESH = pl.DeviceIdType.MESH
GROUP = 4


def chunks_of(depth):
    return 4 if depth % 512 == 0 else 1


def matmul(left, right, precision=lax.Precision.HIGHEST):
    return jnp.dot(left, right, precision=precision, preferred_element_type=jnp.float32)


def greet_all(count):
    row, me = lax.axis_index("prow"), lax.axis_index("pcol")
    barrier = pltpu.get_barrier_semaphore()
    for step in range(1, count):
        pl.semaphore_signal(barrier, inc=1, device_id=(row, lax.rem(me + step, count)), device_id_type=MESH)
    pl.semaphore_wait(barrier, count - 1)


def place_of(line, plane, piece):
    reach = line - 2
    return jnp.clip(plane, piece - reach, piece + reach)


def split(value):
    coarse = value.astype(jnp.bfloat16)
    return coarse, (value - coarse.astype(jnp.float32)).astype(jnp.bfloat16)


def spread_kernel(
    line, slab_ref, vec_ref, xr, vall, y_ref,
    xtile, vtile, xsend, xrecv, vright, vleft, vrecv, own_sem, xload, vload,
):
    count = line * GROUP
    row, me = lax.axis_index("prow"), lax.axis_index("pcol")
    z, q = me // GROUP, lax.rem(me, GROUP)
    depth = vec_ref.shape[0]
    chunks = chunks_of(depth)
    part = depth // chunks
    greet_all(count)

    def vcopy(source, chunk, to, src, sems):
        rows = pl.ds(pl.multiple_of(chunk * part, part), part)
        return pltpu.make_async_remote_copy(
            src_ref=src.at[rows, :],
            dst_ref=vall.at[source, rows, :],
            send_sem=sems.at[source, chunk],
            recv_sem=vrecv.at[source, chunk],
            device_id=(row, to * GROUP + q),
            device_id_type=MESH,
        )

    for chunk in range(chunks):
        @pl.when(z < line - 1)
        def _():
            vcopy(z, chunk, z + 1, vec_ref, vright).start()

        @pl.when(z > 0)
        def _():
            vcopy(z, chunk, z - 1, vec_ref, vleft).start()

    own = pltpu.make_async_copy(vec_ref, vall.at[z], own_sem)
    own.start()

    def xcopy(piece, step):
        other = lax.rem(q + step, GROUP)
        place = place_of(line, z, piece)
        slot = jnp.where(place == z, piece, line)
        columns = pl.ds(pl.multiple_of((piece * GROUP + other) * depth, 128), depth)
        return place, other, slot, columns

    def xremote(piece, step):
        place, other, slot, columns = xcopy(piece, step)
        return pltpu.make_async_remote_copy(
            src_ref=slab_ref.at[:, columns],
            dst_ref=xr.at[slot, q],
            send_sem=xsend.at[piece, step],
            recv_sem=xrecv.at[slot, q],
            device_id=(row, place * GROUP + other),
            device_id_type=MESH,
        )

    def xlocal(piece):
        _, _, _, columns = xcopy(piece, 0)
        return pltpu.make_async_copy(slab_ref.at[:, columns], xr.at[piece, q], xrecv.at[piece, q])

    def far(piece):
        return place_of(line, z, piece) != z

    for step in (1, 2, 3, 0):
        for piece in range(line):
            if step:
                xremote(piece, step).start()
            else:
                @pl.when(far(piece))
                def _():
                    xremote(piece, 0).start()

                @pl.when(jnp.logical_not(far(piece)))
                def _():
                    xlocal(piece).start()

    for distance in range(1, line - 2):
        for chunk in range(chunks):
            @pl.when(z - distance >= 0)
            def _():
                source = z - distance
                vcopy(source, chunk, z, vall.at[source], vright).wait_recv()

                @pl.when(z < line - 1)
                def _():
                    vcopy(source, chunk, z + 1, vall.at[source], vright).start()

            @pl.when(z + distance <= line - 1)
            def _():
                source = z + distance
                vcopy(source, chunk, z, vall.at[source], vleft).wait_recv()

                @pl.when(z > 0)
                def _():
                    vcopy(source, chunk, z - 1, vall.at[source], vleft).start()

    own.wait()

    def xarrived(slot, other):
        pltpu.make_async_remote_copy(
            src_ref=xr.at[slot, other],
            dst_ref=xr.at[slot, other],
            send_sem=xsend.at[0, 0],
            recv_sem=xrecv.at[slot, other],
            device_id=(row, me),
            device_id_type=MESH,
        ).wait_recv()

    for piece in range(line):
        @pl.when(jnp.logical_not(far(piece)))
        def _():
            xlocal(piece).wait()
            for step in range(1, GROUP):
                xarrived(piece, lax.rem(q + step, GROUP))

    def load(slot, piece, chunk):
        span = pl.ds(pl.multiple_of(chunk * part, part), part)
        return (
            pltpu.make_async_copy(xr.at[slot, :, :, span], xtile, xload),
            pltpu.make_async_copy(vall.at[piece, span, :], vtile, vload),
        )

    def accumulate(kind):
        left, left_fine = split(xtile[...].reshape(GROUP * xtile.shape[1], part))
        right, right_fine = split(vtile[...])
        dot = functools.partial(jnp.dot, preferred_element_type=jnp.float32)
        y_ref[kind] += dot(left, right) + (dot(left_fine, right) + dot(left, right_fine))

    y_ref[...] = jnp.zeros_like(y_ref)

    def near_body(index, carry):
        piece = index // chunks

        @pl.when(jnp.logical_and(piece - z < line - 2, z - piece < line - 2))
        def _():
            loads = load(piece, piece, lax.rem(index, chunks))
            for copy in loads:
                copy.start()
            for copy in loads:
                copy.wait()
            accumulate(0)

        return carry

    lax.fori_loop(0, line * chunks, near_body, 0)

    helps = jnp.logical_or(z == 1, z == line - 2)

    @pl.when(helps)
    def _():
        for other in range(GROUP):
            xarrived(line, other)

    @pl.when(jnp.logical_or(z <= 1, z >= line - 2))
    def _():
        last = jnp.where(z <= 1, z + line - 2, z - line + 2)

        def last_body(chunk, carry):
            vcopy(last, chunk, z, vec_ref, vright).wait_recv()
            loads = load(last, last, chunk)
            for copy in loads:
                copy.start()
            for copy in loads:
                copy.wait()
            accumulate(0)

            @pl.when(helps)
            def _():
                span = pl.ds(pl.multiple_of(chunk * part, part), part)
                again = pltpu.make_async_copy(xr.at[line, :, :, span], xtile, xload)
                again.start()
                again.wait()
                accumulate(1)

            return carry

        lax.fori_loop(0, chunks, last_body, 0)

    for piece in range(line):
        for step in range(1, GROUP):
            xremote(piece, step).wait_send()

        @pl.when(far(piece))
        def _():
            xremote(piece, 0).wait_send()

    for distance in range(0, line - 2):
        for chunk in range(chunks):
            @pl.when(jnp.logical_and(z - distance >= 0, z < line - 1))
            def _():
                vcopy(z - distance, chunk, z + 1, vec_ref, vright).wait_send()

            @pl.when(jnp.logical_and(z + distance <= line - 1, z > 0))
            def _():
                vcopy(z + distance, chunk, z - 1, vec_ref, vleft).wait_send()


def spread(line, slab, vectors):
    rows = slab.shape[0]
    depth, width = vectors.shape
    chunks = chunks_of(depth)
    return pl.pallas_call(
        functools.partial(spread_kernel, line),
        out_shape=(
            jax.ShapeDtypeStruct((line + 1, GROUP, rows, depth), jnp.float32),
            jax.ShapeDtypeStruct((line, depth, width), jnp.float32),
            jax.ShapeDtypeStruct((2, GROUP * rows, width), jnp.float32),
        ),
        in_specs=[pl.BlockSpec(memory_space=pl.ANY)] * 2,
        out_specs=(pl.BlockSpec(memory_space=pl.ANY),) * 2 + (pl.BlockSpec(memory_space=pltpu.VMEM),),
        scratch_shapes=[
            pltpu.VMEM((GROUP, rows, depth // chunks), jnp.float32),
            pltpu.VMEM((depth // chunks, width), jnp.float32),
            pltpu.SemaphoreType.DMA((line, GROUP)),
            pltpu.SemaphoreType.DMA((line + 1, GROUP)),
            pltpu.SemaphoreType.DMA((line, chunks)),
            pltpu.SemaphoreType.DMA((line, chunks)),
            pltpu.SemaphoreType.DMA((line, chunks)),
            pltpu.SemaphoreType.DMA,
            pltpu.SemaphoreType.DMA,
            pltpu.SemaphoreType.DMA,
        ],
        compiler_params=pltpu.CompilerParams(
            collective_id=0, has_side_effects=True, vmem_limit_bytes=40 * 1024 * 1024
        ),
        name="spread",
    )(slab, vectors)


def across(left, right):
    return lax.dot_general(left, right, (((1,), (1,)), ((), ())), preferred_element_type=jnp.float32)


def finish_kernel(
    line, lanes, x_ref, v_ref, y_ref, gram_ref, t_ref, out_ref,
    xbuf, vbuf, inbox, total, wbox, wsplit,
    xload, vload, ysend, yrecv, wsend, wrecv, send, recv, handed,
):
    row, me = lax.axis_index("prow"), lax.axis_index("pcol")
    z, q = me // GROUP, lax.rem(me, GROUP)
    members = lanes * GROUP
    mine = row * GROUP + q
    blocks, width = t_ref.shape[0], t_ref.shape[1]
    rows, depth = xbuf.shape[2], xbuf.shape[3]
    share = GROUP * rows // members

    helps = jnp.logical_or(z == 1, z == line - 2)
    ends = jnp.logical_or(z == 0, z == line - 1)
    low = z <= 1
    far_plane = jnp.where(low, 0, line - 1)
    far_piece = jnp.where(low, line - 1, 0)
    help_plane = jnp.where(low, 1, line - 2)
    partner = jnp.where(ends, help_plane, far_plane)

    def device(plane, member):
        return (member // GROUP, plane * GROUP + lax.rem(member, GROUP))

    def others():
        return [lax.rem(mine + step, members) for step in range(1, members)]

    def near(piece):
        return place_of(line, z, piece) == z

    def xarrive(slot):
        return pltpu.make_async_copy(x_ref.at[slot], xbuf.at[slot], xload.at[slot])

    for slot in range(line + 1):
        @pl.when(near(slot) if slot < line else helps)
        def _():
            xarrive(slot).start()

    for piece in range(line):
        pltpu.make_async_copy(v_ref.at[piece], vbuf.at[piece], vload.at[piece]).start()

    barrier = pltpu.get_barrier_semaphore()
    for other in others():
        pl.semaphore_signal(barrier, inc=1, device_id=device(z, other), device_id_type=MESH)

    @pl.when(jnp.logical_or(helps, ends))
    def _():
        for other in range(members):
            pl.semaphore_signal(barrier, inc=1, device_id=device(partner, other), device_id_type=MESH)

    pl.semaphore_wait(barrier, members - 1 + jnp.where(jnp.logical_or(helps, ends), members, 0))

    def strip(member):
        return pl.ds(pl.multiple_of(member * share, share), share)

    def ycopy(kind, plane, member):
        return pltpu.make_async_remote_copy(
            src_ref=y_ref.at[kind, strip(member), :],
            dst_ref=inbox.at[kind * members + mine],
            send_sem=ysend.at[kind * members + member],
            recv_sem=yrecv.at[kind * members + mine],
            device_id=device(plane, member),
            device_id_type=MESH,
        )

    def yarrived(index):
        pltpu.make_async_remote_copy(
            src_ref=inbox.at[index],
            dst_ref=inbox.at[index],
            send_sem=ysend.at[0],
            recv_sem=yrecv.at[index],
            device_id=(row, me),
            device_id_type=MESH,
        ).wait_recv()

    @pl.when(helps)
    def _():
        for other in range(members):
            ycopy(1, far_plane, other).start()

    for other in others():
        ycopy(0, z, other).start()

    total[...] = y_ref[0, strip(mine), :]
    for other in others():
        yarrived(other)
        total[...] += inbox[other]

    @pl.when(ends)
    def _():
        for other in range(members):
            yarrived(members + other)
            total[...] += inbox[members + other]

    done = {}
    for k in reversed(range(blocks)):
        now = total[:, k * width : (k + 1) * width]
        for j in done:
            now = now - matmul(done[j], gram_ref[(j - 1) * width : j * width, k * width : (k + 1) * width])
        done[k] = lax.dot_general(
            now, t_ref[k], (((1,), (1,)), ((), ())),
            precision=lax.Precision.HIGHEST, preferred_element_type=jnp.float32,
        )
    for k in range(blocks):
        wbox[0, strip(mine), k * width : (k + 1) * width] = done[k]

    def wcopy(kind, plane, member):
        return pltpu.make_async_remote_copy(
            src_ref=wbox.at[0, strip(mine), :],
            dst_ref=wbox.at[kind, strip(mine), :],
            send_sem=wsend.at[kind * members + member],
            recv_sem=wrecv.at[kind * members + mine],
            device_id=device(plane, member),
            device_id_type=MESH,
        )

    def warrived(kind, member):
        pltpu.make_async_remote_copy(
            src_ref=wbox.at[kind, strip(member), :],
            dst_ref=wbox.at[kind, strip(member), :],
            send_sem=wsend.at[0],
            recv_sem=wrecv.at[kind * members + member],
            device_id=(row, me),
            device_id_type=MESH,
        ).wait_recv()

    @pl.when(ends)
    def _():
        for other in range(members):
            wcopy(1, help_plane, other).start()

    for other in others():
        wcopy(0, z, other).start()

    for slot in range(line + 1):
        @pl.when(near(slot) if slot < line else helps)
        def _():
            xarrive(slot).wait()

    for piece in range(line):
        pltpu.make_async_copy(v_ref.at[piece], vbuf.at[piece], vload.at[piece]).wait()

    tile = 512 if depth % 512 == 0 else depth

    def update(slot, piece, kind):
        def body(index, carry):
            span = pl.ds(pl.multiple_of(index * tile, tile), tile)
            coarse, fine = split(vbuf[piece, span, :])
            first, second = wsplit[2 * kind], wsplit[2 * kind + 1]
            change = across(first, coarse) + (across(second, coarse) + across(first, fine))
            for group in range(GROUP):
                xbuf[slot, group, :, span] = (
                    xbuf[slot, group, :, span] - change[group * rows : (group + 1) * rows]
                )
            return carry

        lax.fori_loop(0, depth // tile, body, 0)

    def columns(piece, other):
        return pl.ds(pl.multiple_of((piece * GROUP + other) * depth, 128), depth)

    def remote(piece, other):
        return pltpu.make_async_remote_copy(
            src_ref=xbuf.at[piece, other],
            dst_ref=out_ref.at[:, columns(piece, q)],
            send_sem=send.at[piece, other],
            recv_sem=recv.at[piece, q],
            device_id=(row, z * GROUP + other),
            device_id_type=MESH,
        )

    def local(piece):
        return pltpu.make_async_copy(xbuf.at[piece, q], out_ref.at[:, columns(piece, q)], recv.at[piece, q])

    def hand(group, plane):
        return pltpu.make_async_remote_copy(
            src_ref=xbuf.at[line, group],
            dst_ref=xbuf.at[far_piece, group],
            send_sem=send.at[line, group],
            recv_sem=handed.at[group],
            device_id=(row, plane * GROUP + q),
            device_id_type=MESH,
        )

    @pl.when(helps)
    def _():
        for other in range(members):
            warrived(1, other)
        wsplit[2], wsplit[3] = split(wbox[1])
        update(line, far_piece, 1)
        for group in range(GROUP):
            hand(group, far_plane).start()

    for other in others():
        warrived(0, other)
    wsplit[0], wsplit[1] = split(wbox[0])

    for piece in range(line):
        @pl.when(near(piece))
        def _():
            update(piece, piece, 0)
            for step in (1, 2, 3):
                remote(piece, lax.rem(q + step, GROUP)).start()
            local(piece).start()

    @pl.when(ends)
    def _():
        for group in range(GROUP):
            hand(group, z).wait_recv()

            @pl.when(q == group)
            def _():
                local(far_piece).start()

            @pl.when(q != group)
            def _():
                remote(far_piece, group).start()

    def arrived(piece, other):
        pltpu.make_async_remote_copy(
            src_ref=xbuf.at[0, 0],
            dst_ref=out_ref.at[:, columns(piece, other)],
            send_sem=send.at[0, 0],
            recv_sem=recv.at[piece, other],
            device_id=(row, me),
            device_id_type=MESH,
        ).wait_recv()

    for piece in range(line):
        local(piece).wait()
        for step in range(1, GROUP):
            arrived(piece, lax.rem(q + step, GROUP))
            remote(piece, lax.rem(q + step, GROUP)).wait_send()

    for other in others():
        ycopy(0, z, other).wait_send()
        wcopy(0, z, other).wait_send()

    @pl.when(ends)
    def _():
        for other in range(members):
            wcopy(1, help_plane, other).wait_send()

    @pl.when(helps)
    def _():
        for other in range(members):
            ycopy(1, far_plane, other).wait_send()
        for group in range(GROUP):
            hand(group, far_plane).wait_send()


def finish(line, lanes, x, v, y, gram, tfactors):
    _, _, rows, depth = x.shape
    total = v.shape[2]
    members = lanes * GROUP
    share = GROUP * rows // members
    dma = pltpu.SemaphoreType.DMA
    return pl.pallas_call(
        functools.partial(finish_kernel, line, lanes),
        out_shape=jax.ShapeDtypeStruct((rows, line * GROUP * depth), jnp.float32),
        in_specs=[pl.BlockSpec(memory_space=pl.ANY)] * 2 + [pl.BlockSpec(memory_space=pltpu.VMEM)] * 3,
        out_specs=pl.BlockSpec(memory_space=pl.ANY),
        scratch_shapes=[
            pltpu.VMEM(x.shape, jnp.float32),
            pltpu.VMEM(v.shape, jnp.float32),
            pltpu.VMEM((2 * members, share, total), jnp.float32),
            pltpu.VMEM((share, total), jnp.float32),
            pltpu.VMEM((2, GROUP * rows, total), jnp.float32),
            pltpu.VMEM((4, GROUP * rows, total), jnp.bfloat16),
            dma((line + 1,)),
            dma((line,)),
            dma((2 * members,)),
            dma((2 * members,)),
            dma((2 * members,)),
            dma((2 * members,)),
            dma((line + 1, GROUP)),
            dma((line, GROUP)),
            dma((GROUP,)),
        ],
        compiler_params=pltpu.CompilerParams(
            collective_id=1, has_side_effects=True, vmem_limit_bytes=60 * 1024 * 1024
        ),
        name="finish",
    )(x, v, y, gram, tfactors)


def per_device(line, lanes, slab, vectors, tfactors):
    width = tfactors.shape[1]
    gram = lax.psum(matmul(vectors[:, width:].T, vectors[:, :-width], lax.Precision.HIGH), ("prow", "pcol"))
    blocks, vall, products = spread(line, slab, vectors)
    return finish(line, lanes, blocks, vall, products, gram, tfactors)


def solution(mesh):
    line = mesh.shape["pcol"] // GROUP
    lanes = mesh.shape["prow"]
    in_specs = (P("pcol", "prow"), P(("prow", "pcol"), None), P())
    out_specs = P("pcol", "prow")
    return jax.shard_map(
        functools.partial(per_device, line, lanes),
        mesh=mesh, in_specs=in_specs, out_specs=out_specs, check_vma=False,
    )
```
